32 devices in a mesh: parts: 2 (over y), dp: 4 (over z), clu: 2 (over x), sub: 2 (over core).
Axes of the slice: x: 2, y: 2, z: 4, core: 2. Of those that a mesh axis runs over, the one named last changes fastest.
Arguments:
- embeddings: bfloat16 [8192, 4096], P(('parts', 'dp', 'clu'), 'sub'), parts along dimension 0, may hold values from -20 to 20
- projection: bfloat16 [4096, 512], P('sub'), may hold values from -0.09375 to 0.09375
- cluster_ids: int32 [8192], P(('parts', 'dp', 'clu', 'sub')), parts along dimension 0, may hold values from 0 to 7, as said below
Outputs:
- dup_scores: float32 [8192], P(('parts', 'dp', 'clu', 'sub')), parts along dimension 0
The draws below stay inside these ranges and needn't reach their ends.
There are 2 independent parts, one for each index of `parts`. The reference program is written for one: setup_inputs(seed, part) draws one part's arguments, and reference() takes and returns one part's arrays. A program takes and returns all parts, laid end to end along the dimension named above; an argument that names none is the same for every part. Nothing has to cross between parts.
Inputs may be any that keep to these rules, and one draw needn't show every extreme that they name: `cluster_ids`: in each aligned block of 256 rows (the rows of one device) no cluster id appears more than 128 times, and some id appears exactly 128 times.
All inputs are finite; a program needn't handle non-finite values.
Results may differ from the reference program's by a relative error of at most 0.0003.
Values may be sent and summed in bfloat16 or wider, within the bound.
A program may use at most 64 MiB of HBM per device.

```python
import math
import jax
import jax.numpy as jnp
from jax import lax

W = 4096
SK = 512
ROW_DEV = 256
CLUSTERS = 8
CAP = 128
ROWS = 4096
N_DP = 4
N_CLU = 2
N_SUB = 2


def cluster_table(key):
    key_busy, key_forced, key_noise, key_order = jax.random.split(key, 4)
    position_count = CLUSTERS * CAP
    blocks = ROWS // ROW_DEV
    busy_count = max(1, CLUSTERS // 8)
    occupied_flag = (jax.random.permutation(key_busy, CLUSTERS) < busy_count).astype(jnp.int32)
    compelled_choice = jax.random.randint(key_forced, (blocks, 1), 0, CLUSTERS)
    position_cluster = jnp.arange(position_count, dtype=jnp.int32) // CAP
    reward_term = occupied_flag[position_cluster][None, :] * 16384 + (position_cluster[None, :] == compelled_choice).astype(jnp.int32) * 131072
    random_jitter = jax.random.randint(key_noise, (blocks, position_count), 0, 32768)
    ranking_score = (random_jitter + reward_term) * position_count + jnp.arange(position_count, dtype=jnp.int32)[None, :]
    chosen = lax.top_k(ranking_score, ROW_DEV)[1].astype(jnp.int32)
    shuffle_keys = jax.random.randint(key_order, (blocks, ROW_DEV), 0, 1048576) * ROW_DEV + jnp.arange(ROW_DEV, dtype=jnp.int32)[None, :]
    shuffle = jnp.argsort(shuffle_keys, axis=1)
    chosen = jnp.take_along_axis(chosen, shuffle, axis=1)
    return (chosen // CAP).reshape(ROWS).astype(jnp.int32)


def draw_cluster_ids(key, part):
    table = cluster_table(key)
    return table


def draw_embeddings(key, part):
    table = cluster_table(key)
    key = jax.random.fold_in(key, 7)
    key_center, key_noise, key_amp, key_sub, key_ident, key_pick, key_group = jax.random.split(key, 7)
    group_size = max(1, ROWS // CLUSTERS)
    sub_count = 16
    sub_pick = jax.random.randint(key_pick, (ROWS,), 0, sub_count)
    group_pick = jax.random.randint(key_group, (ROWS,), 0, group_size)
    sub_row = table * sub_count + sub_pick
    ident_row = table * group_size + group_pick
    centers = jnp.clip(jax.random.normal(key_center, (CLUSTERS, W), jnp.float32), -4.0, 4.0)
    sub_centers = jnp.clip(jax.random.normal(key_sub, (CLUSTERS * sub_count, W), jnp.float32), -4.0, 4.0)
    identities = jnp.clip(jax.random.normal(key_ident, (CLUSTERS * group_size, W), jnp.float32), -4.0, 4.0)
    random_jitter = jnp.clip(jax.random.normal(key_noise, (ROWS, W), jnp.float32), -4.0, 4.0)
    amplitude = jnp.exp(jax.random.uniform(key_amp, (ROWS, 1), jnp.float32, math.log(0.15), math.log(2.5)))
    values = amplitude * centers[table] + 0.7 * sub_centers[sub_row] + 1.5 * identities[ident_row] + 0.3 * random_jitter
    return jnp.clip(values, -20.0, 20.0).astype(jnp.bfloat16)


def level_of(own_key, dims, cuts, least, top_value):
    def one(dim, shards_of):
        heights = jax.random.uniform(jax.random.fold_in(jax.random.fold_in(own_key, 6), dim), (shards_of,), jnp.float32, least / len(cuts), top_value / len(cuts))
        return jnp.repeat(jnp.exp(heights), dims[dim] // shards_of).reshape((-1,) + (1,) * (len(dims) - dim - 1))

    gain = one(*cuts[0])
    for cut in cuts[1:]:
        gain = gain * one(*cut)
    return gain


def gaussian(rng, shape, scale, reach, cuts=(), kind=jnp.bfloat16):
    drawn = jax.random.normal(rng, shape, jnp.float32) * scale
    if len(cuts) > 0:
        drawn = level_of(rng, shape, cuts, -0.22, 0.18) * drawn
    return jnp.clip(drawn, min=-reach, max=reach).astype(kind)


def setup_inputs(seed: int = 0, part: int = 0) -> dict:
    keys = jax.random.split(jax.random.key(seed), 4)
    part_splits = jax.random.split(jax.random.fold_in(keys[3], part), 4)
    return {
        "embeddings": draw_embeddings(jax.random.fold_in(jax.random.fold_in(keys[3], part), 71), part),
        "projection": gaussian(keys[1], (W, SK), W ** -0.5, 0.09375, ((0, 2),)),
        "cluster_ids": draw_cluster_ids(jax.random.fold_in(jax.random.fold_in(keys[3], part), 71), part),
    }


sharpness = 10.0
level = 0.5

def reference(embeddings, projection, cluster_ids):
    sketch = jnp.dot(embeddings, projection, preferred_element_type=jnp.float32)
    scale = lax.rsqrt(lax.optimization_barrier(jnp.mean(sketch * sketch, axis=1, keepdims=True)) + 1e-06) / math.sqrt(SK)
    unit = (sketch * scale).astype(jnp.bfloat16)
    cluster_span = N_DP * N_CLU * N_SUB * CAP
    tile_rows = min(512, cluster_span)
    tile_count = cluster_span // tile_rows
    sort_order = jnp.argsort(cluster_ids, stable=True).astype(jnp.int32)
    sorted_ids = cluster_ids[sort_order]
    sorted_unit = unit[sort_order]
    padded = jnp.concatenate([sorted_unit, jnp.zeros((cluster_span, SK), jnp.bfloat16)], axis=0)
    counts = lax.optimization_barrier(jnp.sum((cluster_ids[:, None] == jnp.arange(CLUSTERS, dtype=jnp.int32)[None, :]).astype(jnp.int32), axis=0)).astype(jnp.int32)
    starts = (jnp.cumsum(counts) - counts).astype(jnp.int32)
    position = jnp.arange(cluster_span, dtype=jnp.int32)

    def cluster_sums(pair):
        offset, member_count = pair
        cluster_rows = lax.dynamic_slice_in_dim(padded, offset, cluster_span, 0)
        live_mask = (position < member_count).astype(jnp.float32)
        pieces = []
        for query_tile in range(tile_count):
            query_rows = cluster_rows[query_tile * tile_rows:(query_tile + 1) * tile_rows]
            query_pos = position[query_tile * tile_rows:(query_tile + 1) * tile_rows]

            def live_rows(carry, query_rows=query_rows, query_pos=query_pos):
                running = carry
                for key_tile in range(tile_count):
                    key_block = cluster_rows[key_tile * tile_rows:(key_tile + 1) * tile_rows]
                    key_pos = position[key_tile * tile_rows:(key_tile + 1) * tile_rows]
                    key_live = live_mask[key_tile * tile_rows:(key_tile + 1) * tile_rows]

                    def add_tile(acc, key_block=key_block, key_pos=key_pos, key_live=key_live):
                        cosine = jnp.dot(query_rows, key_block.T, preferred_element_type=jnp.float32)
                        weight = jax.nn.sigmoid(sharpness * (cosine - level)) * key_live[None, :]
                        weight = jnp.where(query_pos[:, None] == key_pos[None, :], jnp.float32(0.0), weight)
                        return acc + lax.optimization_barrier(jnp.sum(weight, axis=1))
                    running = lax.cond(key_tile * tile_rows < member_count, add_tile, lambda acc: acc, running)
                return running
            empty = jnp.zeros((tile_rows,), jnp.float32)
            pieces.append(lax.cond(query_tile * tile_rows < member_count, live_rows, lambda carry: carry, empty))
        return jnp.concatenate(pieces)
    totals = lax.map(cluster_sums, (starts, counts))
    row_pos = (jnp.arange(ROWS, dtype=jnp.int32) - starts[sorted_ids]).astype(jnp.int32)
    sorted_scores = jnp.log1p(totals[sorted_ids, row_pos])
    return jnp.zeros((ROWS,), jnp.float32).at[sort_order].set(sorted_scores)
```

```python
import math

import jax
import jax.numpy as jnp
from jax import lax
from jax.experimental import pallas as pl
from jax.experimental.pallas import tpu as pltpu
from jax.sharding import PartitionSpec as P

sharpness = 10.0
level = 0.5

MESH = pl.DeviceIdType.MESH
PARTIAL_CHUNKS = 2
CHUNKS = 4
ROUTES = ((1, (2, 3)), (3, (2,)), (0, (1, 2, 3)))
FIRST, DOWN, LAST = 0, 1, 2


def is_any(z, levels):
    out = z == levels[0]
    for other in levels[1:]:
        out = out | (z == other)
    return out


def pair_kernel(
    emb_ref, proj_ref, ids_ref, out_ref,
    emb, proj, outgoing, incoming, mine,
    peers, keys, peer_ids, key_ids, key_cols, own_cols,
    row_sums, row_recv, key_sums, col_send, col_recv,
    load_sem, part_send, part_recv, ids_send, ids_recv, kid_send, kid_recv,
    peer_send, peer_recv, key_send, key_recv, row_ssem, row_rsem, col_ssem, col_rsem,
):
    x, z, s = lax.axis_index("clu"), lax.axis_index("dp"), lax.axis_index("sub")
    rows, width = mine.shape
    depth = proj.shape[0]
    target = {
        1: {"sub": 1 - s},
        2: {"clu": 1 - x},
        3: {"clu": 1 - x, "sub": 1 - s},
    }

    barrier = pltpu.get_barrier_semaphore()
    for r in (1, 2, 3):
        pl.semaphore_signal(barrier, inc=1, device_id=target[r], device_id_type=MESH)
        pl.semaphore_signal(
            barrier, inc=1, device_id={"dp": lax.rem(z + r, 4)}, device_id_type=MESH
        )

    half = depth // 2
    loads = []

    def load(src, dst):
        copy = pltpu.make_async_copy(src, dst, load_sem.at[len(loads)])
        copy.start()
        loads.append(copy)

    peer_rows = pl.ds(pl.multiple_of((1 - s) * rows, rows), rows)
    own_rows = pl.ds(pl.multiple_of(s * rows, rows), rows)
    for h in range(2):
        cut = pl.ds(h * half, half)
        load(proj_ref.at[cut, :], proj.at[cut, :])
        load(emb_ref.at[peer_rows, cut], emb.at[0, :, cut])
    load(emb_ref.at[own_rows, :], emb.at[1])

    ids = jnp.broadcast_to(ids_ref[...].astype(jnp.float32), (8, rows))
    peer_ids[0] = ids

    def columns(block):
        return jnp.transpose(jnp.broadcast_to(block[0:1, :], (128, rows)))

    own_cols[...] = columns(ids)

    def remote(src, dst, send, recv, device):
        return pltpu.make_async_remote_copy(
            src_ref=src, dst_ref=dst, send_sem=send, recv_sem=recv,
            device_id=device, device_id_type=MESH,
        )

    part_rows = rows // PARTIAL_CHUNKS

    def partial(c):
        cut = pl.ds(c * part_rows, part_rows)
        return remote(
            outgoing.at[cut], incoming.at[cut], part_send.at[c], part_recv.at[c], target[1]
        )

    def ids_copy(r):
        return remote(peer_ids.at[0], peer_ids.at[r], ids_send.at[r], ids_recv.at[r], target[r])

    def key_ids_copy(k, j):
        return remote(
            peer_ids.at[0], key_ids.at[k], kid_send.at[j], kid_recv.at[k],
            {"dp": ROUTES[k][1][j]},
        )

    step = rows // CHUNKS

    def peer_copy(r, c):
        cut = pl.ds(c * step, step)
        return remote(
            peers.at[2 if r == 3 else 0, cut], peers.at[r, cut],
            peer_send.at[r, c], peer_recv.at[r, c], target[2 if r == 2 else 1],
        )

    def key_copy(k, c, origin):
        cut = pl.ds(c * step, step)
        to = z - 1 if k == DOWN else z + 1
        src = peers.at[0, cut] if origin else keys.at[k, cut]
        return remote(src, keys.at[k, cut], key_send.at[k, c], key_recv.at[k, c], {"dp": to})

    def rows_copy(r):
        return remote(row_sums.at[r], row_recv.at[r], row_ssem.at[r], row_rsem.at[r], target[r])

    def cols_copy(k, j):
        return remote(
            col_send.at[k], col_recv.at[j], col_ssem.at[k], col_rsem.at[j], {"dp": ROUTES[k][0]}
        )

    loads[0].wait()
    loads[1].wait()
    outgoing[...] = jnp.dot(
        emb[0, :, 0:half], proj[0:half, :], preferred_element_type=jnp.float32
    )
    loads[2].wait()
    loads[3].wait()
    pl.semaphore_wait(barrier, 6)
    for r in (1, 2, 3):
        ids_copy(r).start()
    for k, (source, levels) in enumerate(ROUTES):

        @pl.when(z == source)
        def _():
            for j in range(len(levels)):
                key_ids_copy(k, j).start()

    for c in range(PARTIAL_CHUNKS):
        cut = pl.ds(c * part_rows, part_rows)
        outgoing[cut, :] += jnp.dot(
            emb[0, cut, half:depth], proj[half:depth, :], preferred_element_type=jnp.float32
        )
        partial(c).start()
    loads[4].wait()
    mine[...] = jnp.dot(emb[1], proj[...], preferred_element_type=jnp.float32)

    for c in range(PARTIAL_CHUNKS):
        cut = pl.ds(c * part_rows, part_rows)
        partial(c).wait_recv()
        sketch = mine[cut, :] + incoming[cut, :]
        scale = lax.rsqrt(
            jnp.mean(sketch * sketch, axis=1, keepdims=True) + 1e-06
        ) / math.sqrt(width)
        peers[0, cut, :] = (sketch * scale).astype(jnp.bfloat16)
        for d in range(c * CHUNKS // PARTIAL_CHUNKS, (c + 1) * CHUNKS // PARTIAL_CHUNKS):
            for k, (source, _levels) in enumerate(ROUTES):

                @pl.when(z == source)
                def _():
                    key_copy(k, d, True).start()

            peer_copy(2, d).start()
            peer_copy(1, d).start()

    def double_weights(block, block_cols, r):
        cosine = lax.dot_general(
            block, peers[r], (((1,), (1,)), ((), ())), preferred_element_type=jnp.float32
        )
        twice = 1.0 + jnp.tanh((0.5 * sharpness) * cosine - (0.5 * sharpness * level))
        cols = jnp.concatenate([block_cols] * (rows // 128), axis=1)
        return jnp.where(cols == peer_ids[r, 0:1, :], twice, 0.0)

    def fold_lanes(weights):
        out = weights[:, 0:128]
        for t in range(1, rows // 128):
            out = out + weights[:, t * 128 : (t + 1) * 128]
        return out

    def fold_rows(weights):
        return jnp.sum(weights.reshape(weights.shape[0] // 8, 8, weights.shape[1]), axis=0)

    own = double_weights(peers[0], own_cols[...], 0)
    row_id = lax.broadcasted_iota(jnp.int32, (rows, rows), 0)
    col_id = lax.broadcasted_iota(jnp.int32, (rows, rows), 1)
    mine[:, 0:128] = fold_lanes(jnp.where(row_id == col_id, 0.0, own))

    for r in (1, 2, 3):
        ids_copy(r).wait_recv()
    for k, (source, levels) in enumerate(ROUTES):

        @pl.when(is_any(z, levels))
        def _():
            key_ids_copy(k, 0).wait_recv()
            key_cols[k] = columns(key_ids[k])

    for c in range(CHUNKS):

        @pl.when(z == 1)
        def _():
            key_copy(LAST, c, False).wait_recv()
            key_copy(LAST, c, False).start()

        @pl.when(z == 2)
        def _():
            key_copy(FIRST, c, False).wait_recv()
            key_copy(FIRST, c, False).start()

        peer_copy(2, c).wait_recv()
        peer_copy(3, c).start()
        if c == 0:
            for d in range(CHUNKS):
                peer_copy(1, d).wait_recv()
            mine[:, 0:128] += fold_lanes(double_weights(peers[0], own_cols[...], 1))

    mine[:, 0:128] += fold_lanes(double_weights(peers[0], own_cols[...], 2))
    for c in range(CHUNKS):
        peer_copy(3, c).wait_recv()
    mine[:, 0:128] += fold_lanes(double_weights(peers[0], own_cols[...], 3))
    out_ref[...] = fold_rows(jnp.transpose(mine[:, 0:128]))
    row_sums[...] = jnp.zeros_like(row_sums)

    def meet(k, start, count):
        cut = pl.ds(start, count)
        block, cols = keys[k, cut, :], key_cols[k, cut, :]
        total = None
        for r in range(4):
            weights = double_weights(block, cols, r)
            row_sums[r] += fold_rows(weights)
            lanes = fold_lanes(weights)
            total = lanes if total is None else total + lanes
        key_sums[cut, :] = total

    def give_back(k):
        col_send[k] = fold_rows(jnp.transpose(key_sums[...]))
        for j, there in enumerate(ROUTES[k][1]):

            @pl.when(z == there)
            def _():
                cols_copy(k, j).start()

    @pl.when(z >= 2)
    def _():
        @pl.when(z == 3)
        def _():
            for c in range(CHUNKS):
                key_copy(FIRST, c, False).wait_recv()

        meet(FIRST, 0, rows)
        give_back(FIRST)

    @pl.when(z == 2)
    def _():
        for c in range(CHUNKS):
            key_copy(DOWN, c, False).wait_recv()
        meet(DOWN, 0, rows)
        give_back(DOWN)

    @pl.when(z >= 1)
    def _():
        for c in range(CHUNKS):

            @pl.when(z >= 2)
            def _():
                key_copy(LAST, c, False).wait_recv()

            @pl.when(z == 2)
            def _():
                key_copy(LAST, c, False).start()

            meet(LAST, c * step, step)
        for r in (1, 2, 3):
            rows_copy(r).start()
        give_back(LAST)
        out_ref[...] += row_sums[0]
        for r in (1, 2, 3):
            rows_copy(r).wait_recv()
            out_ref[...] += row_recv[r]

    for k, (source, levels) in enumerate(ROUTES):

        @pl.when(z == source)
        def _():
            for j in range(len(levels)):
                cols_copy(k, j).wait_recv()
                out_ref[...] += col_recv[j]

    for c in range(PARTIAL_CHUNKS):
        partial(c).wait_send()
    for r in (1, 2, 3):
        ids_copy(r).wait_send()
        for c in range(CHUNKS):
            peer_copy(r, c).wait_send()

    @pl.when(z >= 1)
    def _():
        for r in (1, 2, 3):
            rows_copy(r).wait_send()

    for k, (source, levels) in enumerate(ROUTES):

        @pl.when(z == source)
        def _():
            for j in range(len(levels)):
                key_ids_copy(k, j).wait_send()

        @pl.when(is_any(z, (source,) + levels[:-1]))
        def _():
            for c in range(CHUNKS):
                key_copy(k, c, True).wait_send()

        @pl.when(is_any(z, levels))
        def _():
            cols_copy(k, 0).wait_send()


def all_pairs(embeddings, projection, cluster_ids):
    rows = cluster_ids.shape[0]
    depth, width = projection.shape
    dma = pltpu.SemaphoreType.DMA
    f32, bf16 = jnp.float32, jnp.bfloat16
    doubled = pl.pallas_call(
        pair_kernel,
        out_shape=jax.ShapeDtypeStruct((8, rows), f32),
        in_specs=[
            pl.BlockSpec(memory_space=pl.ANY),
            pl.BlockSpec(memory_space=pl.ANY),
            pl.BlockSpec(memory_space=pltpu.VMEM),
        ],
        out_specs=pl.BlockSpec(memory_space=pltpu.VMEM),
        scratch_shapes=[
            pltpu.VMEM((2, rows, depth), bf16),
            pltpu.VMEM((depth, width), bf16),
            pltpu.VMEM((rows, width), f32),
            pltpu.VMEM((rows, width), f32),
            pltpu.VMEM((rows, width), f32),
            pltpu.VMEM((4, rows, width), bf16),
            pltpu.VMEM((3, rows, width), bf16),
            pltpu.VMEM((4, 8, rows), f32),
            pltpu.VMEM((3, 8, rows), f32),
            pltpu.VMEM((3, rows, 128), f32),
            pltpu.VMEM((rows, 128), f32),
            pltpu.VMEM((4, 8, rows), f32),
            pltpu.VMEM((4, 8, rows), f32),
            pltpu.VMEM((rows, 128), f32),
            pltpu.VMEM((3, 8, rows), f32),
            pltpu.VMEM((3, 8, rows), f32),
            dma((5,)),
            dma((PARTIAL_CHUNKS,)),
            dma((PARTIAL_CHUNKS,)),
            dma((4,)),
            dma((4,)),
            dma((3,)),
            dma((3,)),
            dma((4, CHUNKS)),
            dma((4, CHUNKS)),
            dma((3, CHUNKS)),
            dma((3, CHUNKS)),
            dma((4,)),
            dma((4,)),
            dma((3,)),
            dma((3,)),
        ],
        compiler_params=pltpu.CompilerParams(
            collective_id=0, has_side_effects=True, vmem_limit_bytes=32 * 1024 * 1024
        ),
        cost_estimate=pl.CostEstimate(
            flops=2 * (2 * rows) * depth * width + 2 * 16 * rows * rows * width,
            bytes_accessed=4 * rows * depth + 2 * depth * width,
            transcendentals=16 * rows * rows,
        ),
    )(embeddings, projection, cluster_ids.reshape(1, rows))
    return jnp.log1p(0.5 * jnp.sum(doubled, axis=0))


def pair_weights(queries, key_rows):
    cosine = jnp.einsum("qc,kc->qk", queries, key_rows, preferred_element_type=jnp.float32)
    return jax.nn.sigmoid(sharpness * (cosine - level))


def routed(embeddings, projection, cluster_ids):
    row_count = cluster_ids.shape[0]
    sketch_width = projection.shape[1]
    owners = lax.axis_size("dp") * lax.axis_size("clu")
    capacity = max(8, 4 * row_count // owners)
    position_count = owners * capacity
    sketch = lax.psum_scatter(
        jnp.dot(embeddings, projection, preferred_element_type=jnp.float32),
        "sub",
        scatter_dimension=0,
        tiled=True,
    )
    scale = lax.rsqrt(jnp.mean(sketch * sketch, axis=1, keepdims=True) + 1e-06) / math.sqrt(
        sketch_width
    )
    unit = (sketch * scale).astype(jnp.bfloat16)
    same_cluster = cluster_ids[:, None] == cluster_ids[None, :]
    row_iota = jnp.arange(row_count, dtype=jnp.int32)
    earlier = row_iota[:, None] > row_iota[None, :]
    slot_rank = jnp.sum((same_cluster & earlier).astype(jnp.int32), axis=1)
    slot_index = cluster_ids * capacity + slot_rank
    outbox = jnp.zeros((position_count, sketch_width), jnp.bfloat16).at[slot_index].set(unit)
    filled = (
        jnp.zeros((position_count,), jnp.bfloat16)
        .at[slot_index]
        .set(jnp.ones((row_count,), jnp.bfloat16))
    )
    inbox, live = (
        lax.all_to_all(
            outbox.reshape(owners, capacity, sketch_width),
            ("dp", "clu"),
            split_axis=0,
            concat_axis=0,
            tiled=True,
        ),
        lax.all_to_all(
            filled.reshape(owners, capacity), ("dp", "clu"), split_axis=0, concat_axis=0, tiled=True
        ),
    )
    inbox = inbox.reshape(position_count, sketch_width)
    core_index = lax.axis_index("sub")
    local_index = jnp.arange(position_count, dtype=jnp.int32)
    block_rows = min(512, position_count)
    own_index = core_index * position_count + local_index
    key_rows = lax.all_gather(inbox, "sub", axis=0, tiled=True)
    key_flags = lax.all_gather(live.reshape(position_count), "sub", axis=0, tiled=True)
    key_index = jnp.arange(key_rows.shape[0], dtype=jnp.int32)
    key_live = key_flags.astype(jnp.float32)

    def one_block(args):
        queries, query_index = args
        weight = pair_weights(queries, key_rows) * key_live[None, :]
        weight = jnp.where(query_index[:, None] == key_index[None, :], jnp.float32(0.0), weight)
        return jnp.sum(weight, axis=1)

    row_sums = lax.map(
        one_block, (inbox.reshape(-1, block_rows, sketch_width), own_index.reshape(-1, block_rows))
    )
    totals = row_sums.reshape(position_count)
    slot_scores = jnp.log1p(totals)
    returned = lax.all_to_all(
        slot_scores.reshape(owners, capacity),
        ("dp", "clu"),
        split_axis=0,
        concat_axis=0,
        tiled=True,
    )
    return returned.reshape(position_count)[slot_index]


def solution(mesh):
    in_specs = (P(("parts", "dp", "clu"), "sub"), P("sub", None), P(("parts", "dp", "clu", "sub")))
    out_specs = P(("parts", "dp", "clu", "sub"))
    sizes = tuple(mesh.shape[name] for name in ("dp", "clu", "sub"))
    per_device = all_pairs if sizes == (4, 2, 2) else routed
    return jax.shard_map(
        per_device, mesh=mesh, in_specs=in_specs, out_specs=out_specs, check_vma=False
    )
```

```python
import math

import jax
import jax.numpy as jnp
from jax import lax
from jax.experimental import pallas as pl
from jax.experimental.pallas import tpu as pltpu
from jax.sharding import PartitionSpec as P

sharpness = 10.0
level = 0.5

MESH = pl.DeviceIdType.MESH
PARTIAL_CHUNKS = 2
CHUNKS = 4
DETOUR = (0, 1)
DIRECT = tuple(c for c in range(CHUNKS) if c not in DETOUR)
ROUTES = ((1, (2, 3)), (3, (2,)), (0, (1, 2, 3)))
FIRST, DOWN, LAST = 0, 1, 2


def is_any(z, levels):
    out = z == levels[0]
    for other in levels[1:]:
        out = out | (z == other)
    return out


def pair_kernel(
    emb_ref, proj_ref, ids_ref, out_ref,
    emb, proj, outgoing, incoming, mine,
    peers, keys, transit, peer_ids, key_ids, key_cols, own_cols, own_total,
    row_sums, row_recv, key_sums, col_send, col_recv,
    load_sem, part_send, part_recv, ids_send, ids_recv, kid_send, kid_recv,
    peer_send, peer_recv, key_send, key_recv, row_ssem, row_rsem, col_ssem, col_rsem,
    way_send, way_recv, home_send,
):
    x, s, p = lax.axis_index("clu"), lax.axis_index("sub"), lax.axis_index("parts")
    height = lax.axis_index("dp")
    up = 1 - 2 * p
    z = height + p * (3 - 2 * height)
    partner = {"parts": 1 - p}

    def lane(there):
        return {"dp": there + p * (3 - 2 * there)}

    rows, width = mine.shape
    depth = proj.shape[0]
    target = {
        1: {"sub": 1 - s},
        2: {"clu": 1 - x},
        3: {"clu": 1 - x, "sub": 1 - s},
    }

    barrier = pltpu.get_barrier_semaphore()
    for r in (1, 2, 3):
        pl.semaphore_signal(barrier, inc=1, device_id=target[r], device_id_type=MESH)
        pl.semaphore_signal(
            barrier, inc=1, device_id={"dp": lax.rem(height + r, 4)}, device_id_type=MESH
        )
    pl.semaphore_signal(barrier, inc=1, device_id=partner, device_id_type=MESH)

    half = depth // 2
    loads = []

    def load(src, dst):
        copy = pltpu.make_async_copy(src, dst, load_sem.at[len(loads)])
        copy.start()
        loads.append(copy)

    peer_rows = pl.ds(pl.multiple_of((1 - s) * rows, rows), rows)
    own_rows = pl.ds(pl.multiple_of(s * rows, rows), rows)
    for h in range(2):
        cut = pl.ds(h * half, half)
        load(proj_ref.at[cut, :], proj.at[cut, :])
        load(emb_ref.at[peer_rows, cut], emb.at[0, :, cut])
    load(emb_ref.at[own_rows, :], emb.at[1])

    ids = jnp.broadcast_to(ids_ref[...].astype(jnp.float32), (8, rows))
    peer_ids[0] = ids

    def columns(block):
        return jnp.transpose(jnp.broadcast_to(block[0:1, :], (128, rows)))

    own_cols[...] = columns(ids)

    def remote(src, dst, send, recv, device):
        return pltpu.make_async_remote_copy(
            src_ref=src, dst_ref=dst, send_sem=send, recv_sem=recv,
            device_id=device, device_id_type=MESH,
        )

    part_rows = rows // PARTIAL_CHUNKS

    def partial(c):
        cut = pl.ds(c * part_rows, part_rows)
        return remote(
            outgoing.at[cut], incoming.at[cut], part_send.at[c], part_recv.at[c], target[1]
        )

    def ids_copy(r):
        return remote(peer_ids.at[0], peer_ids.at[r], ids_send.at[r], ids_recv.at[r], target[r])

    def key_ids_copy(k, j):
        return remote(
            peer_ids.at[0], key_ids.at[k], kid_send.at[j], kid_recv.at[k],
            lane(ROUTES[k][1][j]),
        )

    step = rows // CHUNKS

    def peer_copy(r, c):
        cut = pl.ds(c * step, step)
        return remote(
            peers.at[2 if r == 3 else 0, cut], peers.at[r, cut],
            peer_send.at[r, c], peer_recv.at[r, c], target[2 if r == 2 else 1],
        )

    def key_copy(k, c, origin):
        cut = pl.ds(c * step, step)
        to = height - up if k == DOWN else height + up
        src = peers.at[0, cut] if origin else keys.at[k, cut]
        return remote(src, keys.at[k, cut], key_send.at[k, c], key_recv.at[k, c], {"dp": to})

    def way_copy(c, out):
        cut = pl.ds(c * step, step)
        return remote(
            peers.at[0, cut] if out else transit.at[cut], transit.at[cut],
            way_send.at[0 if out else 1, c], way_recv.at[c], partner if out else {"dp": height - up},
        )

    def home_copy(c):
        cut = pl.ds(c * step, step)
        return remote(
            transit.at[cut], keys.at[FIRST, cut], home_send.at[c], key_recv.at[FIRST, c], partner
        )

    def rows_copy(r):
        return remote(row_sums.at[r], row_recv.at[r], row_ssem.at[r], row_rsem.at[r], target[r])

    def cols_copy(k, j):
        return remote(
            col_send.at[k], col_recv.at[j], col_ssem.at[k], col_rsem.at[j], lane(ROUTES[k][0])
        )

    loads[0].wait()
    loads[1].wait()
    outgoing[...] = jnp.dot(
        emb[0, :, 0:half], proj[0:half, :], preferred_element_type=jnp.float32
    )
    loads[2].wait()
    loads[3].wait()
    pl.semaphore_wait(barrier, 7)
    for c in range(PARTIAL_CHUNKS):
        cut = pl.ds(c * part_rows, part_rows)
        outgoing[cut, :] += jnp.dot(
            emb[0, cut, half:depth], proj[half:depth, :], preferred_element_type=jnp.float32
        )
        partial(c).start()
    for r in (1, 2, 3):
        ids_copy(r).start()
    for k, (source, levels) in enumerate(ROUTES):

        @pl.when(z == source)
        def _():
            for j in range(len(levels)):
                key_ids_copy(k, j).start()

    loads[4].wait()
    mine[...] = jnp.dot(emb[1], proj[...], preferred_element_type=jnp.float32)

    for c in range(PARTIAL_CHUNKS):
        cut = pl.ds(c * part_rows, part_rows)
        partial(c).wait_recv()
        sketch = mine[cut, :] + incoming[cut, :]
        scale = lax.rsqrt(
            jnp.mean(sketch * sketch, axis=1, keepdims=True) + 1e-06
        ) / math.sqrt(width)
        peers[0, cut, :] = (sketch * scale).astype(jnp.bfloat16)
        for d in range(c * CHUNKS // PARTIAL_CHUNKS, (c + 1) * CHUNKS // PARTIAL_CHUNKS):
            for k, (source, _levels) in enumerate(ROUTES):

                @pl.when(z == source)
                def _():
                    if k == FIRST and d in DETOUR:
                        way_copy(d, True).start()
                    else:
                        key_copy(k, d, True).start()

            peer_copy(2, d).start()
            peer_copy(1, d).start()

    def double_weights(block, block_cols, r):
        cosine = lax.dot_general(
            block, peers[r], (((1,), (1,)), ((), ())), preferred_element_type=jnp.float32
        )
        twice = 1.0 + jnp.tanh((0.5 * sharpness) * cosine - (0.5 * sharpness * level))
        cols = jnp.concatenate([block_cols] * (rows // 128), axis=1)
        return jnp.where(cols == peer_ids[r, 0:1, :], twice, 0.0)

    def fold_lanes(weights):
        out = weights[:, 0:128]
        for t in range(1, rows // 128):
            out = out + weights[:, t * 128 : (t + 1) * 128]
        return out

    def fold_rows(weights):
        return jnp.sum(weights.reshape(weights.shape[0] // 8, 8, weights.shape[1]), axis=0)

    def own_pairs(r):
        weights = double_weights(peers[0], own_cols[...], r)
        if r == 0:
            row_id = lax.broadcasted_iota(jnp.int32, (rows, rows), 0)
            col_id = lax.broadcasted_iota(jnp.int32, (rows, rows), 1)
            mine[:, 0:128] = fold_lanes(jnp.where(row_id == col_id, 0.0, weights))
        else:
            mine[:, 0:128] += fold_lanes(weights)

    def pass_transit(c):
        way_copy(c, False).wait_recv()

        @pl.when(z >= 1)
        def _():
            way_copy(c, False).start()

        @pl.when(z <= 1)
        def _():
            home_copy(c).start()

    for c in range(CHUNKS):

        @pl.when(z == 1)
        def _():
            key_copy(LAST, c, False).wait_recv()
            key_copy(LAST, c, False).start()

        if c < len(DETOUR):

            @pl.when(z == 2)
            def _():
                pass_transit(DETOUR[c])

        if c < len(DIRECT):

            @pl.when(z == 2)
            def _():
                key_copy(FIRST, DIRECT[c], False).wait_recv()
                key_copy(FIRST, DIRECT[c], False).start()

        if 0 <= c - 1 < len(DETOUR):

            @pl.when(z == 1)
            def _():
                pass_transit(DETOUR[c - 1])

        peer_copy(2, c).wait_recv()
        peer_copy(3, c).start()
        if c == 0:
            for r in (1, 2, 3):
                ids_copy(r).wait_recv()
            own_pairs(0)
        if c == 1:
            for d in range(CHUNKS):
                peer_copy(1, d).wait_recv()
            own_pairs(1)

    @pl.when(z == 0)
    def _():
        for c in DETOUR:
            pass_transit(c)

    for k, (source, levels) in enumerate(ROUTES):

        @pl.when(is_any(z, levels))
        def _():
            key_ids_copy(k, 0).wait_recv()
            key_cols[k] = columns(key_ids[k])

    own_pairs(2)
    for c in range(CHUNKS):
        peer_copy(3, c).wait_recv()
    own_pairs(3)
    own_total[...] = fold_rows(jnp.transpose(mine[:, 0:128]))
    row_sums[...] = jnp.zeros_like(row_sums)

    def meet(k, start, count):
        cut = pl.ds(start, count)
        block, cols = keys[k, cut, :], key_cols[k, cut, :]
        total = None
        for r in range(4):
            weights = double_weights(block, cols, r)
            row_sums[r] += fold_rows(weights)
            lanes = fold_lanes(weights)
            total = lanes if total is None else total + lanes
        key_sums[k, cut, :] = total

    def give_back(k):
        col_send[k] = fold_rows(jnp.transpose(key_sums[k]))
        for j, there in enumerate(ROUTES[k][1]):

            @pl.when(z == there)
            def _():
                cols_copy(k, j).start()

    @pl.when(z >= 2)
    def _():
        for c in DIRECT:

            @pl.when(z == 3)
            def _():
                key_copy(FIRST, c, False).wait_recv()

            meet(FIRST, c * step, step)

    @pl.when(z == 2)
    def _():
        for c in range(CHUNKS):
            key_copy(DOWN, c, False).wait_recv()
        meet(DOWN, 0, rows)
        give_back(DOWN)

    @pl.when(z >= 1)
    def _():
        for c in range(CHUNKS):

            @pl.when(z >= 2)
            def _():
                key_copy(LAST, c, False).wait_recv()

            @pl.when(z == 2)
            def _():
                key_copy(LAST, c, False).start()

            meet(LAST, c * step, step)
            if 0 <= c - 1 < len(DETOUR):
                d = DETOUR[c - 1]

                @pl.when(z >= 2)
                def _():
                    home_copy(d).wait_recv()
                    meet(FIRST, d * step, step)
                    if d == DETOUR[-1]:
                        give_back(FIRST)

        for r in (1, 2, 3):
            rows_copy(r).start()
        give_back(LAST)
        own_total[...] += row_sums[0]
        for r in (1, 2, 3):
            rows_copy(r).wait_recv()
            own_total[...] += row_recv[r]

    for k, (source, levels) in enumerate(ROUTES):

        @pl.when(z == source)
        def _():
            for j in range(len(levels)):
                cols_copy(k, j).wait_recv()
                own_total[...] += col_recv[j]

    out_ref[...] = jnp.sum(own_total[...], axis=0, keepdims=True)

    for c in range(PARTIAL_CHUNKS):
        partial(c).wait_send()
    for r in (1, 2, 3):
        ids_copy(r).wait_send()
        for c in range(CHUNKS):
            peer_copy(r, c).wait_send()

    @pl.when(z >= 1)
    def _():
        for r in (1, 2, 3):
            rows_copy(r).wait_send()

    for k, (source, levels) in enumerate(ROUTES):

        @pl.when(z == source)
        def _():
            for j in range(len(levels)):
                key_ids_copy(k, j).wait_send()

        @pl.when(is_any(z, (source,) + levels[:-1]))
        def _():
            for c in DIRECT if k == FIRST else range(CHUNKS):
                key_copy(k, c, True).wait_send()

        @pl.when(is_any(z, levels))
        def _():
            cols_copy(k, 0).wait_send()

    for c in DETOUR:

        @pl.when(z == 1)
        def _():
            way_copy(c, True).wait_send()

        @pl.when(is_any(z, (1, 2)))
        def _():
            way_copy(c, False).wait_send()

        @pl.when(z <= 1)
        def _():
            home_copy(c).wait_send()


def all_pairs(embeddings, projection, cluster_ids):
    rows = cluster_ids.shape[0]
    depth, width = projection.shape
    dma = pltpu.SemaphoreType.DMA
    f32, bf16 = jnp.float32, jnp.bfloat16
    doubled = pl.pallas_call(
        pair_kernel,
        out_shape=jax.ShapeDtypeStruct((1, rows), f32),
        in_specs=[
            pl.BlockSpec(memory_space=pl.ANY),
            pl.BlockSpec(memory_space=pl.ANY),
            pl.BlockSpec(memory_space=pltpu.VMEM),
        ],
        out_specs=pl.BlockSpec(memory_space=pltpu.VMEM),
        scratch_shapes=[
            pltpu.VMEM((2, rows, depth), bf16),
            pltpu.VMEM((depth, width), bf16),
            pltpu.VMEM((rows, width), f32),
            pltpu.VMEM((rows, width), f32),
            pltpu.VMEM((rows, width), f32),
            pltpu.VMEM((4, rows, width), bf16),
            pltpu.VMEM((3, rows, width), bf16),
            pltpu.VMEM((rows, width), bf16),
            pltpu.VMEM((4, 8, rows), f32),
            pltpu.VMEM((3, 8, rows), f32),
            pltpu.VMEM((3, rows, 128), f32),
            pltpu.VMEM((rows, 128), f32),
            pltpu.VMEM((8, rows), f32),
            pltpu.VMEM((4, 8, rows), f32),
            pltpu.VMEM((4, 8, rows), f32),
            pltpu.VMEM((3, rows, 128), f32),
            pltpu.VMEM((3, 8, rows), f32),
            pltpu.VMEM((3, 8, rows), f32),
            dma((5,)),
            dma((PARTIAL_CHUNKS,)),
            dma((PARTIAL_CHUNKS,)),
            dma((4,)),
            dma((4,)),
            dma((3,)),
            dma((3,)),
            dma((4, CHUNKS)),
            dma((4, CHUNKS)),
            dma((3, CHUNKS)),
            dma((3, CHUNKS)),
            dma((4,)),
            dma((4,)),
            dma((3,)),
            dma((3,)),
            dma((2, CHUNKS)),
            dma((CHUNKS,)),
            dma((CHUNKS,)),
        ],
        compiler_params=pltpu.CompilerParams(
            collective_id=0, has_side_effects=True, vmem_limit_bytes=60 * 1024 * 1024
        ),
        cost_estimate=pl.CostEstimate(
            flops=2 * (2 * rows) * depth * width + 2 * 16 * rows * rows * width,
            bytes_accessed=4 * rows * depth + 2 * depth * width,
            transcendentals=16 * rows * rows,
        ),
    )(embeddings, projection, cluster_ids.reshape(1, rows))
    return jnp.log1p(0.5 * doubled).reshape(rows)


def pair_weights(queries, key_rows):
    cosine = jnp.einsum("qc,kc->qk", queries, key_rows, preferred_element_type=jnp.float32)
    return jax.nn.sigmoid(sharpness * (cosine - level))


def routed(embeddings, projection, cluster_ids):
    row_count = cluster_ids.shape[0]
    sketch_width = projection.shape[1]
    owners = lax.axis_size("dp") * lax.axis_size("clu")
    capacity = max(8, 4 * row_count // owners)
    position_count = owners * capacity
    sketch = lax.psum_scatter(
        jnp.dot(embeddings, projection, preferred_element_type=jnp.float32),
        "sub",
        scatter_dimension=0,
        tiled=True,
    )
    scale = lax.rsqrt(jnp.mean(sketch * sketch, axis=1, keepdims=True) + 1e-06) / math.sqrt(
        sketch_width
    )
    unit = (sketch * scale).astype(jnp.bfloat16)
    same_cluster = cluster_ids[:, None] == cluster_ids[None, :]
    row_iota = jnp.arange(row_count, dtype=jnp.int32)
    earlier = row_iota[:, None] > row_iota[None, :]
    slot_rank = jnp.sum((same_cluster & earlier).astype(jnp.int32), axis=1)
    slot_index = cluster_ids * capacity + slot_rank
    outbox = jnp.zeros((position_count, sketch_width), jnp.bfloat16).at[slot_index].set(unit)
    filled = (
        jnp.zeros((position_count,), jnp.bfloat16)
        .at[slot_index]
        .set(jnp.ones((row_count,), jnp.bfloat16))
    )
    inbox, live = (
        lax.all_to_all(
            outbox.reshape(owners, capacity, sketch_width),
            ("dp", "clu"),
            split_axis=0,
            concat_axis=0,
            tiled=True,
        ),
        lax.all_to_all(
            filled.reshape(owners, capacity), ("dp", "clu"), split_axis=0, concat_axis=0, tiled=True
        ),
    )
    inbox = inbox.reshape(position_count, sketch_width)
    core_index = lax.axis_index("sub")
    local_index = jnp.arange(position_count, dtype=jnp.int32)
    block_rows = min(512, position_count)
    own_index = core_index * position_count + local_index
    key_rows = lax.all_gather(inbox, "sub", axis=0, tiled=True)
    key_flags = lax.all_gather(live.reshape(position_count), "sub", axis=0, tiled=True)
    key_index = jnp.arange(key_rows.shape[0], dtype=jnp.int32)
    key_live = key_flags.astype(jnp.float32)

    def one_block(args):
        queries, query_index = args
        weight = pair_weights(queries, key_rows) * key_live[None, :]
        weight = jnp.where(query_index[:, None] == key_index[None, :], jnp.float32(0.0), weight)
        return jnp.sum(weight, axis=1)

    row_sums = lax.map(
        one_block, (inbox.reshape(-1, block_rows, sketch_width), own_index.reshape(-1, block_rows))
    )
    totals = row_sums.reshape(position_count)
    slot_scores = jnp.log1p(totals)
    returned = lax.all_to_all(
        slot_scores.reshape(owners, capacity),
        ("dp", "clu"),
        split_axis=0,
        concat_axis=0,
        tiled=True,
    )
    return returned.reshape(position_count)[slot_index]


def solution(mesh):
    in_specs = (P(("parts", "dp", "clu"), "sub"), P("sub", None), P(("parts", "dp", "clu", "sub")))
    out_specs = P(("parts", "dp", "clu", "sub"))
    sizes = tuple(mesh.shape[name] for name in ("dp", "clu", "sub"))
    per_device = all_pairs if sizes == (4, 2, 2) else routed
    return jax.shard_map(
        per_device, mesh=mesh, in_specs=in_specs, out_specs=out_specs, check_vma=False
    )
```

```python
import math

import jax
import jax.numpy as jnp
from jax import lax
from jax.experimental import pallas as pl
from jax.experimental.pallas import tpu as pltpu
from jax.sharding import PartitionSpec as P

sharpness = 10.0
level = 0.5

MESH = pl.DeviceIdType.MESH
PARTIAL_CHUNKS = 2
CHUNKS = 4
ROUTES = ((1, (2, 3)), (3, (2,)), (0, (1, 2, 3)))
FIRST, DOWN, LAST = 0, 1, 2


def is_any(z, levels):
    out = z == levels[0]
    for other in levels[1:]:
        out = out | (z == other)
    return out


def pair_kernel(
    emb_ref, proj_ref, ids_ref, out_ref,
    emb, proj, outgoing, incoming, mine,
    peers, keys, peer_ids, key_ids, key_cols, own_cols, total_ref,
    row_sums, row_recv, key_sums, col_send, col_recv,
    load_sem, part_send, part_recv, ids_send, ids_recv, kid_send, kid_recv,
    peer_send, peer_recv, key_send, key_recv, row_ssem, row_rsem, col_ssem, col_rsem,
):
    x, z, s = lax.axis_index("clu"), lax.axis_index("dp"), lax.axis_index("sub")
    rows, width = mine.shape
    depth = proj.shape[0]
    target = {
        1: {"sub": 1 - s},
        2: {"clu": 1 - x},
        3: {"clu": 1 - x, "sub": 1 - s},
    }

    barrier = pltpu.get_barrier_semaphore()
    for r in (1, 2, 3):
        pl.semaphore_signal(barrier, inc=1, device_id=target[r], device_id_type=MESH)
        pl.semaphore_signal(
            barrier, inc=1, device_id={"dp": lax.rem(z + r, 4)}, device_id_type=MESH
        )

    half = depth // 2
    loads = []

    def load(src, dst):
        copy = pltpu.make_async_copy(src, dst, load_sem.at[len(loads)])
        copy.start()
        loads.append(copy)

    peer_rows = pl.ds(pl.multiple_of((1 - s) * rows, rows), rows)
    own_rows = pl.ds(pl.multiple_of(s * rows, rows), rows)
    for h in range(2):
        cut = pl.ds(h * half, half)
        load(proj_ref.at[cut, :], proj.at[cut, :])
        load(emb_ref.at[peer_rows, cut], emb.at[0, :, cut])
    load(emb_ref.at[own_rows, :], emb.at[1])

    ids = jnp.broadcast_to(ids_ref[...].astype(jnp.float32), (8, rows))
    peer_ids[0] = ids

    def columns(block):
        return jnp.transpose(jnp.broadcast_to(block[0:1, :], (128, rows)))

    own_cols[...] = columns(ids)

    def remote(src, dst, send, recv, device):
        return pltpu.make_async_remote_copy(
            src_ref=src, dst_ref=dst, send_sem=send, recv_sem=recv,
            device_id=device, device_id_type=MESH,
        )

    part_rows = rows // PARTIAL_CHUNKS

    def partial(c):
        cut = pl.ds(c * part_rows, part_rows)
        return remote(
            outgoing.at[cut], incoming.at[cut], part_send.at[c], part_recv.at[c], target[1]
        )

    def ids_copy(r):
        return remote(peer_ids.at[0], peer_ids.at[r], ids_send.at[r], ids_recv.at[r], target[r])

    def key_ids_copy(k, j):
        return remote(
            peer_ids.at[0], key_ids.at[k], kid_send.at[j], kid_recv.at[k],
            {"dp": ROUTES[k][1][j]},
        )

    step = rows // CHUNKS

    def peer_copy(r, c):
        cut = pl.ds(c * step, step)
        return remote(
            peers.at[2 if r == 3 else 0, cut], peers.at[r, cut],
            peer_send.at[r, c], peer_recv.at[r, c], target[2 if r == 2 else 1],
        )

    def key_copy(k, c, origin):
        cut = pl.ds(c * step, step)
        to = z - 1 if k == DOWN else z + 1
        src = peers.at[0, cut] if origin else keys.at[k, cut]
        return remote(src, keys.at[k, cut], key_send.at[k, c], key_recv.at[k, c], {"dp": to})

    def rows_copy(r):
        return remote(row_sums.at[r], row_recv.at[r], row_ssem.at[r], row_rsem.at[r], target[r])

    def cols_copy(k, j):
        return remote(
            col_send.at[k], col_recv.at[j], col_ssem.at[k], col_rsem.at[j], {"dp": ROUTES[k][0]}
        )

    loads[0].wait()
    loads[1].wait()
    outgoing[...] = jnp.dot(
        emb[0, :, 0:half], proj[0:half, :], preferred_element_type=jnp.float32
    )
    loads[2].wait()
    loads[3].wait()
    pl.semaphore_wait(barrier, 6)
    for r in (1, 2, 3):
        ids_copy(r).start()
    for k, (source, levels) in enumerate(ROUTES):

        @pl.when(z == source)
        def _():
            for j in range(len(levels)):
                key_ids_copy(k, j).start()

    for c in range(PARTIAL_CHUNKS):
        cut = pl.ds(c * part_rows, part_rows)
        outgoing[cut, :] += jnp.dot(
            emb[0, cut, half:depth], proj[half:depth, :], preferred_element_type=jnp.float32
        )
        partial(c).start()
    loads[4].wait()
    mine[...] = jnp.dot(emb[1], proj[...], preferred_element_type=jnp.float32)

    for c in range(PARTIAL_CHUNKS):
        cut = pl.ds(c * part_rows, part_rows)
        partial(c).wait_recv()
        sketch = mine[cut, :] + incoming[cut, :]
        scale = lax.rsqrt(
            jnp.mean(sketch * sketch, axis=1, keepdims=True) + 1e-06
        ) / math.sqrt(width)
        peers[0, cut, :] = (sketch * scale).astype(jnp.bfloat16)
        for d in range(c * CHUNKS // PARTIAL_CHUNKS, (c + 1) * CHUNKS // PARTIAL_CHUNKS):
            for k, (source, _levels) in enumerate(ROUTES):

                @pl.when(z == source)
                def _():
                    key_copy(k, d, True).start()

            peer_copy(2, d).start()
            peer_copy(1, d).start()

    def double_weights(block, block_cols, r):
        cosine = lax.dot_general(
            block, peers[r], (((1,), (1,)), ((), ())), preferred_element_type=jnp.float32
        )
        twice = 1.0 + jnp.tanh((0.5 * sharpness) * cosine - (0.5 * sharpness * level))
        cols = jnp.concatenate([block_cols] * (rows // 128), axis=1)
        return jnp.where(cols == peer_ids[r, 0:1, :], twice, 0.0)

    def fold_lanes(weights):
        out = weights[:, 0:128]
        for t in range(1, rows // 128):
            out = out + weights[:, t * 128 : (t + 1) * 128]
        return out

    def fold_rows(weights):
        return jnp.sum(weights.reshape(weights.shape[0] // 8, 8, weights.shape[1]), axis=0)

    own = double_weights(peers[0], own_cols[...], 0)
    row_id = lax.broadcasted_iota(jnp.int32, (rows, rows), 0)
    col_id = lax.broadcasted_iota(jnp.int32, (rows, rows), 1)
    mine[:, 0:128] = fold_lanes(jnp.where(row_id == col_id, 0.0, own))

    for r in (1, 2, 3):
        ids_copy(r).wait_recv()
    for k, (source, levels) in enumerate(ROUTES):

        @pl.when(is_any(z, levels))
        def _():
            key_ids_copy(k, 0).wait_recv()
            key_cols[k] = columns(key_ids[k])

    for c in range(CHUNKS):

        @pl.when(z == 1)
        def _():
            key_copy(LAST, c, False).wait_recv()
            key_copy(LAST, c, False).start()

        @pl.when(z == 2)
        def _():
            key_copy(FIRST, c, False).wait_recv()
            key_copy(FIRST, c, False).start()

        peer_copy(2, c).wait_recv()
        peer_copy(3, c).start()
        if c == 0:
            for d in range(CHUNKS):
                peer_copy(1, d).wait_recv()
            mine[:, 0:128] += fold_lanes(double_weights(peers[0], own_cols[...], 1))

    mine[:, 0:128] += fold_lanes(double_weights(peers[0], own_cols[...], 2))
    for c in range(CHUNKS):
        peer_copy(3, c).wait_recv()
    mine[:, 0:128] += fold_lanes(double_weights(peers[0], own_cols[...], 3))
    total_ref[...] = fold_rows(jnp.transpose(mine[:, 0:128]))
    row_sums[...] = jnp.zeros_like(row_sums)

    def meet(k, start, count):
        cut = pl.ds(start, count)
        block, cols = keys[k, cut, :], key_cols[k, cut, :]
        total = None
        for r in range(4):
            weights = double_weights(block, cols, r)
            row_sums[r] += fold_rows(weights)
            lanes = fold_lanes(weights)
            total = lanes if total is None else total + lanes
        key_sums[cut, :] = total

    def give_back(k):
        col_send[k] = fold_rows(jnp.transpose(key_sums[...]))
        for j, there in enumerate(ROUTES[k][1]):

            @pl.when(z == there)
            def _():
                cols_copy(k, j).start()

    @pl.when(z >= 2)
    def _():
        @pl.when(z == 3)
        def _():
            for c in range(CHUNKS):
                key_copy(FIRST, c, False).wait_recv()

        meet(FIRST, 0, rows)
        give_back(FIRST)

    @pl.when(z == 2)
    def _():
        for c in range(CHUNKS):
            key_copy(DOWN, c, False).wait_recv()
        meet(DOWN, 0, rows)
        give_back(DOWN)

    @pl.when(z >= 1)
    def _():
        for c in range(CHUNKS):

            @pl.when(z >= 2)
            def _():
                key_copy(LAST, c, False).wait_recv()

            @pl.when(z == 2)
            def _():
                key_copy(LAST, c, False).start()

            meet(LAST, c * step, step)
        for r in (1, 2, 3):
            rows_copy(r).start()
        give_back(LAST)
        total_ref[...] += row_sums[0]
        for r in (1, 2, 3):
            rows_copy(r).wait_recv()
            total_ref[...] += row_recv[r]

    for k, (source, levels) in enumerate(ROUTES):

        @pl.when(z == source)
        def _():
            for j in range(len(levels)):
                cols_copy(k, j).wait_recv()
                total_ref[...] += col_recv[j]

    out_ref[...] = jnp.sum(total_ref[...], axis=0, keepdims=True)

    for c in range(PARTIAL_CHUNKS):
        partial(c).wait_send()
    for r in (1, 2, 3):
        ids_copy(r).wait_send()
        for c in range(CHUNKS):
            peer_copy(r, c).wait_send()

    @pl.when(z >= 1)
    def _():
        for r in (1, 2, 3):
            rows_copy(r).wait_send()

    for k, (source, levels) in enumerate(ROUTES):

        @pl.when(z == source)
        def _():
            for j in range(len(levels)):
                key_ids_copy(k, j).wait_send()

        @pl.when(is_any(z, (source,) + levels[:-1]))
        def _():
            for c in range(CHUNKS):
                key_copy(k, c, True).wait_send()

        @pl.when(is_any(z, levels))
        def _():
            cols_copy(k, 0).wait_send()


def all_pairs(embeddings, projection, cluster_ids):
    rows = cluster_ids.shape[0]
    depth, width = projection.shape
    dma = pltpu.SemaphoreType.DMA
    f32, bf16 = jnp.float32, jnp.bfloat16
    doubled = pl.pallas_call(
        pair_kernel,
        out_shape=jax.ShapeDtypeStruct((1, rows), f32),
        in_specs=[
            pl.BlockSpec(memory_space=pl.ANY),
            pl.BlockSpec(memory_space=pl.ANY),
            pl.BlockSpec(memory_space=pltpu.VMEM),
        ],
        out_specs=pl.BlockSpec(memory_space=pltpu.VMEM),
        scratch_shapes=[
            pltpu.VMEM((2, rows, depth), bf16),
            pltpu.VMEM((depth, width), bf16),
            pltpu.VMEM((rows, width), f32),
            pltpu.VMEM((rows, width), f32),
            pltpu.VMEM((rows, width), f32),
            pltpu.VMEM((4, rows, width), bf16),
            pltpu.VMEM((3, rows, width), bf16),
            pltpu.VMEM((4, 8, rows), f32),
            pltpu.VMEM((3, 8, rows), f32),
            pltpu.VMEM((3, rows, 128), f32),
            pltpu.VMEM((rows, 128), f32),
            pltpu.VMEM((8, rows), f32),
            pltpu.VMEM((4, 8, rows), f32),
            pltpu.VMEM((4, 8, rows), f32),
            pltpu.VMEM((rows, 128), f32),
            pltpu.VMEM((3, 8, rows), f32),
            pltpu.VMEM((3, 8, rows), f32),
            dma((5,)),
            dma((PARTIAL_CHUNKS,)),
            dma((PARTIAL_CHUNKS,)),
            dma((4,)),
            dma((4,)),
            dma((3,)),
            dma((3,)),
            dma((4, CHUNKS)),
            dma((4, CHUNKS)),
            dma((3, CHUNKS)),
            dma((3, CHUNKS)),
            dma((4,)),
            dma((4,)),
            dma((3,)),
            dma((3,)),
        ],
        compiler_params=pltpu.CompilerParams(
            collective_id=0, has_side_effects=True, vmem_limit_bytes=60 * 1024 * 1024
        ),
        cost_estimate=pl.CostEstimate(
            flops=2 * (2 * rows) * depth * width + 2 * 16 * rows * rows * width,
            bytes_accessed=4 * rows * depth + 2 * depth * width,
            transcendentals=16 * rows * rows,
        ),
    )(embeddings, projection, cluster_ids.reshape(1, rows))
    return jnp.log1p(0.5 * doubled).reshape(rows)


def pair_weights(queries, key_rows):
    cosine = jnp.einsum("qc,kc->qk", queries, key_rows, preferred_element_type=jnp.float32)
    return jax.nn.sigmoid(sharpness * (cosine - level))


def routed(embeddings, projection, cluster_ids):
    row_count = cluster_ids.shape[0]
    sketch_width = projection.shape[1]
    owners = lax.axis_size("dp") * lax.axis_size("clu")
    capacity = max(8, 4 * row_count // owners)
    position_count = owners * capacity
    sketch = lax.psum_scatter(
        jnp.dot(embeddings, projection, preferred_element_type=jnp.float32),
        "sub",
        scatter_dimension=0,
        tiled=True,
    )
    scale = lax.rsqrt(jnp.mean(sketch * sketch, axis=1, keepdims=True) + 1e-06) / math.sqrt(
        sketch_width
    )
    unit = (sketch * scale).astype(jnp.bfloat16)
    same_cluster = cluster_ids[:, None] == cluster_ids[None, :]
    row_iota = jnp.arange(row_count, dtype=jnp.int32)
    earlier = row_iota[:, None] > row_iota[None, :]
    slot_rank = jnp.sum((same_cluster & earlier).astype(jnp.int32), axis=1)
    slot_index = cluster_ids * capacity + slot_rank
    outbox = jnp.zeros((position_count, sketch_width), jnp.bfloat16).at[slot_index].set(unit)
    filled = (
        jnp.zeros((position_count,), jnp.bfloat16)
        .at[slot_index]
        .set(jnp.ones((row_count,), jnp.bfloat16))
    )
    inbox, live = (
        lax.all_to_all(
            outbox.reshape(owners, capacity, sketch_width),
            ("dp", "clu"),
            split_axis=0,
            concat_axis=0,
            tiled=True,
        ),
        lax.all_to_all(
            filled.reshape(owners, capacity), ("dp", "clu"), split_axis=0, concat_axis=0, tiled=True
        ),
    )
    inbox = inbox.reshape(position_count, sketch_width)
    core_index = lax.axis_index("sub")
    local_index = jnp.arange(position_count, dtype=jnp.int32)
    block_rows = min(512, position_count)
    own_index = core_index * position_count + local_index
    key_rows = lax.all_gather(inbox, "sub", axis=0, tiled=True)
    key_flags = lax.all_gather(live.reshape(position_count), "sub", axis=0, tiled=True)
    key_index = jnp.arange(key_rows.shape[0], dtype=jnp.int32)
    key_live = key_flags.astype(jnp.float32)

    def one_block(args):
        queries, query_index = args
        weight = pair_weights(queries, key_rows) * key_live[None, :]
        weight = jnp.where(query_index[:, None] == key_index[None, :], jnp.float32(0.0), weight)
        return jnp.sum(weight, axis=1)

    row_sums = lax.map(
        one_block, (inbox.reshape(-1, block_rows, sketch_width), own_index.reshape(-1, block_rows))
    )
    totals = row_sums.reshape(position_count)
    slot_scores = jnp.log1p(totals)
    returned = lax.all_to_all(
        slot_scores.reshape(owners, capacity),
        ("dp", "clu"),
        split_axis=0,
        concat_axis=0,
        tiled=True,
    )
    return returned.reshape(position_count)[slot_index]


def solution(mesh):
    in_specs = (P(("parts", "dp", "clu"), "sub"), P("sub", None), P(("parts", "dp", "clu", "sub")))
    out_specs = P(("parts", "dp", "clu", "sub"))
    sizes = tuple(mesh.shape[name] for name in ("dp", "clu", "sub"))
    per_device = all_pairs if sizes == (4, 2, 2) else routed
    return jax.shard_map(
        per_device, mesh=mesh, in_specs=in_specs, out_specs=out_specs, check_vma=False
    )
```

```python
import math

import jax
import jax.numpy as jnp
from jax import lax
from jax.experimental import pallas as pl
from jax.experimental.pallas import tpu as pltpu
from jax.sharding import PartitionSpec as P

sharpness = 10.0
level = 0.5

MESH = pl.DeviceIdType.MESH
PARTIAL_CHUNKS = 2
CHUNKS = 4
ROUTES = ((1, (2, 3)), (3, (2,)), (0, (1, 2, 3)))
FIRST, DOWN, LAST = 0, 1, 2


def is_any(z, levels):
    out = z == levels[0]
    for other in levels[1:]:
        out = out | (z == other)
    return out


def pair_kernel(
    emb_ref, proj_ref, ids_ref, out_ref,
    emb, proj, outgoing, incoming, mine,
    peers, keys, peer_ids, key_ids, key_cols, own_cols, total_ref,
    row_sums, row_recv, key_sums, col_send, col_recv,
    load_sem, part_send, part_recv, ids_send, ids_recv, kid_send, kid_recv,
    peer_send, peer_recv, key_send, key_recv, row_ssem, row_rsem, col_ssem, col_rsem,
):
    x, z, s = lax.axis_index("clu"), lax.axis_index("dp"), lax.axis_index("sub")
    rows, width = mine.shape
    depth = proj.shape[0]
    target = {
        1: {"sub": 1 - s},
        2: {"clu": 1 - x},
        3: {"clu": 1 - x, "sub": 1 - s},
    }

    barrier = pltpu.get_barrier_semaphore()
    for r in (1, 2, 3):
        pl.semaphore_signal(barrier, inc=1, device_id=target[r], device_id_type=MESH)
        pl.semaphore_signal(
            barrier, inc=1, device_id={"dp": lax.rem(z + r, 4)}, device_id_type=MESH
        )

    half = depth // 2
    loads = []

    def load(src, dst):
        copy = pltpu.make_async_copy(src, dst, load_sem.at[len(loads)])
        copy.start()
        loads.append(copy)

    peer_rows = pl.ds(pl.multiple_of((1 - s) * rows, rows), rows)
    own_rows = pl.ds(pl.multiple_of(s * rows, rows), rows)
    for h in range(2):
        cut = pl.ds(h * half, half)
        load(proj_ref.at[cut, :], proj.at[cut, :])
        load(emb_ref.at[peer_rows, cut], emb.at[0, :, cut])
    load(emb_ref.at[own_rows, :], emb.at[1])

    ids = jnp.broadcast_to(ids_ref[...].astype(jnp.float32), (8, rows))
    peer_ids[0] = ids

    def columns(block):
        return jnp.transpose(jnp.broadcast_to(block[0:1, :], (128, rows)))

    own_cols[...] = columns(ids)

    def remote(src, dst, send, recv, device):
        return pltpu.make_async_remote_copy(
            src_ref=src, dst_ref=dst, send_sem=send, recv_sem=recv,
            device_id=device, device_id_type=MESH,
        )

    part_rows = rows // PARTIAL_CHUNKS

    def partial(c):
        cut = pl.ds(c * part_rows, part_rows)
        return remote(
            outgoing.at[cut], incoming.at[cut], part_send.at[c], part_recv.at[c], target[1]
        )

    def ids_copy(r):
        return remote(peer_ids.at[0], peer_ids.at[r], ids_send.at[r], ids_recv.at[r], target[r])

    def key_ids_copy(k, j):
        return remote(
            peer_ids.at[0], key_ids.at[k], kid_send.at[j], kid_recv.at[k],
            {"dp": ROUTES[k][1][j]},
        )

    step = rows // CHUNKS

    def peer_copy(r, c):
        cut = pl.ds(c * step, step)
        return remote(
            peers.at[2 if r == 3 else 0, cut], peers.at[r, cut],
            peer_send.at[r, c], peer_recv.at[r, c], target[2 if r == 2 else 1],
        )

    def key_copy(k, c, origin):
        cut = pl.ds(c * step, step)
        to = z - 1 if k == DOWN else z + 1
        src = peers.at[0, cut] if origin else keys.at[k, cut]
        return remote(src, keys.at[k, cut], key_send.at[k, c], key_recv.at[k, c], {"dp": to})

    def rows_copy(r):
        return remote(row_sums.at[r], row_recv.at[r], row_ssem.at[r], row_rsem.at[r], target[r])

    def cols_copy(k, j):
        return remote(
            col_send.at[k], col_recv.at[j], col_ssem.at[k], col_rsem.at[j], {"dp": ROUTES[k][0]}
        )

    loads[0].wait()
    loads[1].wait()
    outgoing[...] = jnp.dot(
        emb[0, :, 0:half], proj[0:half, :], preferred_element_type=jnp.float32
    )
    loads[2].wait()
    loads[3].wait()
    pl.semaphore_wait(barrier, 6)
    for r in (1, 2, 3):
        ids_copy(r).start()
    for k, (source, levels) in enumerate(ROUTES):

        @pl.when(z == source)
        def _():
            for j in range(len(levels)):
                key_ids_copy(k, j).start()

    for c in range(PARTIAL_CHUNKS):
        cut = pl.ds(c * part_rows, part_rows)
        outgoing[cut, :] += jnp.dot(
            emb[0, cut, half:depth], proj[half:depth, :], preferred_element_type=jnp.float32
        )
        partial(c).start()
    loads[4].wait()
    mine[...] = jnp.dot(emb[1], proj[...], preferred_element_type=jnp.float32)

    for c in range(PARTIAL_CHUNKS):
        cut = pl.ds(c * part_rows, part_rows)
        partial(c).wait_recv()
        sketch = mine[cut, :] + incoming[cut, :]
        scale = lax.rsqrt(
            jnp.mean(sketch * sketch, axis=1, keepdims=True) + 1e-06
        ) / math.sqrt(width)
        peers[0, cut, :] = (sketch * scale).astype(jnp.bfloat16)
        for d in range(c * CHUNKS // PARTIAL_CHUNKS, (c + 1) * CHUNKS // PARTIAL_CHUNKS):
            for k, (source, _levels) in enumerate(ROUTES):

                @pl.when(z == source)
                def _():
                    key_copy(k, d, True).start()

            peer_copy(2, d).start()
            peer_copy(1, d).start()

    def double_weights(block, block_cols, r):
        cosine = lax.dot_general(
            block, peers[r], (((1,), (1,)), ((), ())), preferred_element_type=jnp.float32
        )
        twice = 1.0 + jnp.tanh((0.5 * sharpness) * cosine - (0.5 * sharpness * level))
        cols = jnp.concatenate([block_cols] * (rows // 128), axis=1)
        return jnp.where(cols == peer_ids[r, 0:1, :], twice, 0.0)

    def fold_lanes(weights):
        out = weights[:, 0:128]
        for t in range(1, rows // 128):
            out = out + weights[:, t * 128 : (t + 1) * 128]
        return out

    def fold_rows(weights):
        return jnp.sum(weights.reshape(weights.shape[0] // 8, 8, weights.shape[1]), axis=0)

    own = double_weights(peers[0], own_cols[...], 0)
    row_id = lax.broadcasted_iota(jnp.int32, (rows, rows), 0)
    col_id = lax.broadcasted_iota(jnp.int32, (rows, rows), 1)
    mine[:, 0:128] = fold_lanes(jnp.where(row_id == col_id, 0.0, own))

    for r in (1, 2, 3):
        ids_copy(r).wait_recv()
    for k, (source, levels) in enumerate(ROUTES):

        @pl.when(is_any(z, levels))
        def _():
            key_ids_copy(k, 0).wait_recv()
            key_cols[k] = columns(key_ids[k])

    for c in range(CHUNKS):

        @pl.when(z == 1)
        def _():
            key_copy(LAST, c, False).wait_recv()
            key_copy(LAST, c, False).start()

        @pl.when(z == 2)
        def _():
            key_copy(FIRST, c, False).wait_recv()
            key_copy(FIRST, c, False).start()

        peer_copy(2, c).wait_recv()
        peer_copy(3, c).start()
        if c == 0:
            for d in range(CHUNKS):
                peer_copy(1, d).wait_recv()
            mine[:, 0:128] += fold_lanes(double_weights(peers[0], own_cols[...], 1))

    mine[:, 0:128] += fold_lanes(double_weights(peers[0], own_cols[...], 2))
    for c in range(CHUNKS):
        peer_copy(3, c).wait_recv()
    mine[:, 0:128] += fold_lanes(double_weights(peers[0], own_cols[...], 3))
    total_ref[...] = fold_rows(jnp.transpose(mine[:, 0:128]))
    row_sums[...] = jnp.zeros_like(row_sums)

    def meet(k, start, count):
        cut = pl.ds(start, count)
        block, cols = keys[k, cut, :], key_cols[k, cut, :]
        total = None
        for r in range(4):
            weights = double_weights(block, cols, r)
            row_sums[r] += fold_rows(weights)
            lanes = fold_lanes(weights)
            total = lanes if total is None else total + lanes
        key_sums[cut, :] = total

    def give_back(k):
        col_send[k] = fold_rows(jnp.transpose(key_sums[...]))
        for j, there in enumerate(ROUTES[k][1]):

            @pl.when(z == there)
            def _():
                cols_copy(k, j).start()

    @pl.when(z == 2)
    def _():
        for c in range(CHUNKS):
            key_copy(LAST, c, False).wait_recv()
            key_copy(LAST, c, False).start()
            if c == CHUNKS // 2 - 1:
                meet(FIRST, 0, rows)
                give_back(FIRST)
            if c == CHUNKS // 2:
                for d in range(CHUNKS):
                    key_copy(DOWN, d, False).wait_recv()
                meet(DOWN, 0, rows)
                give_back(DOWN)

    @pl.when(z == 3)
    def _():
        for c in range(CHUNKS):
            key_copy(FIRST, c, False).wait_recv()
        meet(FIRST, 0, rows)
        give_back(FIRST)
        for c in range(CHUNKS):
            key_copy(LAST, c, False).wait_recv()

    @pl.when(z >= 1)
    def _():
        meet(LAST, 0, rows)
        for r in (1, 2, 3):
            rows_copy(r).start()
        give_back(LAST)
        total_ref[...] += row_sums[0]
        for r in (1, 2, 3):
            rows_copy(r).wait_recv()
            total_ref[...] += row_recv[r]

    for k, (source, levels) in enumerate(ROUTES):

        @pl.when(z == source)
        def _():
            for j in range(len(levels)):
                cols_copy(k, j).wait_recv()
                total_ref[...] += col_recv[j]

    out_ref[...] = jnp.sum(total_ref[...], axis=0, keepdims=True)

    for c in range(PARTIAL_CHUNKS):
        partial(c).wait_send()
    for r in (1, 2, 3):
        ids_copy(r).wait_send()
        for c in range(CHUNKS):
            peer_copy(r, c).wait_send()

    @pl.when(z >= 1)
    def _():
        for r in (1, 2, 3):
            rows_copy(r).wait_send()

    for k, (source, levels) in enumerate(ROUTES):

        @pl.when(z == source)
        def _():
            for j in range(len(levels)):
                key_ids_copy(k, j).wait_send()

        @pl.when(is_any(z, (source,) + levels[:-1]))
        def _():
            for c in range(CHUNKS):
                key_copy(k, c, True).wait_send()

        @pl.when(is_any(z, levels))
        def _():
            cols_copy(k, 0).wait_send()


def all_pairs(embeddings, projection, cluster_ids):
    rows = cluster_ids.shape[0]
    depth, width = projection.shape
    dma = pltpu.SemaphoreType.DMA
    f32, bf16 = jnp.float32, jnp.bfloat16
    doubled = pl.pallas_call(
        pair_kernel,
        out_shape=jax.ShapeDtypeStruct((1, rows), f32),
        in_specs=[
            pl.BlockSpec(memory_space=pl.ANY),
            pl.BlockSpec(memory_space=pl.ANY),
            pl.BlockSpec(memory_space=pltpu.VMEM),
        ],
        out_specs=pl.BlockSpec(memory_space=pltpu.VMEM),
        scratch_shapes=[
            pltpu.VMEM((2, rows, depth), bf16),
            pltpu.VMEM((depth, width), bf16),
            pltpu.VMEM((rows, width), f32),
            pltpu.VMEM((rows, width), f32),
            pltpu.VMEM((rows, width), f32),
            pltpu.VMEM((4, rows, width), bf16),
            pltpu.VMEM((3, rows, width), bf16),
            pltpu.VMEM((4, 8, rows), f32),
            pltpu.VMEM((3, 8, rows), f32),
            pltpu.VMEM((3, rows, 128), f32),
            pltpu.VMEM((rows, 128), f32),
            pltpu.VMEM((8, rows), f32),
            pltpu.VMEM((4, 8, rows), f32),
            pltpu.VMEM((4, 8, rows), f32),
            pltpu.VMEM((rows, 128), f32),
            pltpu.VMEM((3, 8, rows), f32),
            pltpu.VMEM((3, 8, rows), f32),
            dma((5,)),
            dma((PARTIAL_CHUNKS,)),
            dma((PARTIAL_CHUNKS,)),
            dma((4,)),
            dma((4,)),
            dma((3,)),
            dma((3,)),
            dma((4, CHUNKS)),
            dma((4, CHUNKS)),
            dma((3, CHUNKS)),
            dma((3, CHUNKS)),
            dma((4,)),
            dma((4,)),
            dma((3,)),
            dma((3,)),
        ],
        compiler_params=pltpu.CompilerParams(
            collective_id=0, has_side_effects=True, vmem_limit_bytes=60 * 1024 * 1024
        ),
        cost_estimate=pl.CostEstimate(
            flops=2 * (2 * rows) * depth * width + 2 * 16 * rows * rows * width,
            bytes_accessed=4 * rows * depth + 2 * depth * width,
            transcendentals=16 * rows * rows,
        ),
    )(embeddings, projection, cluster_ids.reshape(1, rows))
    return jnp.log1p(0.5 * doubled).reshape(rows)


def pair_weights(queries, key_rows):
    cosine = jnp.einsum("qc,kc->qk", queries, key_rows, preferred_element_type=jnp.float32)
    return jax.nn.sigmoid(sharpness * (cosine - level))


def routed(embeddings, projection, cluster_ids):
    row_count = cluster_ids.shape[0]
    sketch_width = projection.shape[1]
    owners = lax.axis_size("dp") * lax.axis_size("clu")
    capacity = max(8, 4 * row_count // owners)
    position_count = owners * capacity
    sketch = lax.psum_scatter(
        jnp.dot(embeddings, projection, preferred_element_type=jnp.float32),
        "sub",
        scatter_dimension=0,
        tiled=True,
    )
    scale = lax.rsqrt(jnp.mean(sketch * sketch, axis=1, keepdims=True) + 1e-06) / math.sqrt(
        sketch_width
    )
    unit = (sketch * scale).astype(jnp.bfloat16)
    same_cluster = cluster_ids[:, None] == cluster_ids[None, :]
    row_iota = jnp.arange(row_count, dtype=jnp.int32)
    earlier = row_iota[:, None] > row_iota[None, :]
    slot_rank = jnp.sum((same_cluster & earlier).astype(jnp.int32), axis=1)
    slot_index = cluster_ids * capacity + slot_rank
    outbox = jnp.zeros((position_count, sketch_width), jnp.bfloat16).at[slot_index].set(unit)
    filled = (
        jnp.zeros((position_count,), jnp.bfloat16)
        .at[slot_index]
        .set(jnp.ones((row_count,), jnp.bfloat16))
    )
    inbox, live = (
        lax.all_to_all(
            outbox.reshape(owners, capacity, sketch_width),
            ("dp", "clu"),
            split_axis=0,
            concat_axis=0,
            tiled=True,
        ),
        lax.all_to_all(
            filled.reshape(owners, capacity), ("dp", "clu"), split_axis=0, concat_axis=0, tiled=True
        ),
    )
    inbox = inbox.reshape(position_count, sketch_width)
    core_index = lax.axis_index("sub")
    local_index = jnp.arange(position_count, dtype=jnp.int32)
    block_rows = min(512, position_count)
    own_index = core_index * position_count + local_index
    key_rows = lax.all_gather(inbox, "sub", axis=0, tiled=True)
    key_flags = lax.all_gather(live.reshape(position_count), "sub", axis=0, tiled=True)
    key_index = jnp.arange(key_rows.shape[0], dtype=jnp.int32)
    key_live = key_flags.astype(jnp.float32)

    def one_block(args):
        queries, query_index = args
        weight = pair_weights(queries, key_rows) * key_live[None, :]
        weight = jnp.where(query_index[:, None] == key_index[None, :], jnp.float32(0.0), weight)
        return jnp.sum(weight, axis=1)

    row_sums = lax.map(
        one_block, (inbox.reshape(-1, block_rows, sketch_width), own_index.reshape(-1, block_rows))
    )
    totals = row_sums.reshape(position_count)
    slot_scores = jnp.log1p(totals)
    returned = lax.all_to_all(
        slot_scores.reshape(owners, capacity),
        ("dp", "clu"),
        split_axis=0,
        concat_axis=0,
        tiled=True,
    )
    return returned.reshape(position_count)[slot_index]


def solution(mesh):
    in_specs = (P(("parts", "dp", "clu"), "sub"), P("sub", None), P(("parts", "dp", "clu", "sub")))
    out_specs = P(("parts", "dp", "clu", "sub"))
    sizes = tuple(mesh.shape[name] for name in ("dp", "clu", "sub"))
    per_device = all_pairs if sizes == (4, 2, 2) else routed
    return jax.shard_map(
        per_device, mesh=mesh, in_specs=in_specs, out_specs=out_specs, check_vma=False
    )
```
